1024 devices in a mesh: row: 16 (over y, core), col: 64 (over z, x).
Axes of the slice: x: 8, y: 8, z: 8, core: 2. Of those that a mesh axis runs over, the one named last changes fastest.
Arguments:
- features: bfloat16 [655360, 128], P(('row', 'col')), may hold values from -6 to 6
- send_blocks: int32 [16, 64, 16, 2], P('row', 'col'), may hold values from -1 to 4, as said below
- tile_slots: int32 [16, 64, 20, 4], P('row', 'col'), may hold values from 0 to 31, as said below
- tile_count: int32 [16, 64, 20], P('row', 'col'), may hold values from 1 to 4, as said below
- adjacency: bfloat16 [16, 64, 20, 128, 512], P('row', 'col'), may hold values from -0.25 to 0.25
- w_self: bfloat16 [128, 256], replicated, may hold values from -0.5 to 0.5
- w_neigh: bfloat16 [128, 256], replicated, may hold values from -0.5 to 0.5
- bias: float32 [256], replicated, may hold values from -3 to 3
Outputs:
- hidden: bfloat16 [655360, 256], P(('row', 'col'))
The draws below stay inside these ranges and needn't reach their ends.
Inputs may be any that keep to these rules, and one draw needn't show every extreme that they name: `send_blocks`: each (owner, reader) pair has 1 to 2 live slots, first in order, holding distinct blocks of the owner; the rest are -1; every owner has 2 live slots for some reader. `tile_slots`: each entry names a live slot q * 2 + s of the need-list that owner (q, c) keeps for this device's row on the same col. `tile_count`: every device has a destination block with 4 live tiles.
All inputs are finite; a program needn't handle non-finite values.
Results may differ from the reference program's by a relative error of at most 0.0043.
Values may be sent and summed in bfloat16 or wider, within the bound.
No kernel may reach another device: no remote copies, remote signals or barrier semaphores. Data moves between devices by JAX's collectives and lax.ppermute only.
A program may use at most 32 MiB of HBM per device.

```python
import jax
import jax.numpy as jnp
from jax import lax

F = 128
H = 256
TILE = 128
NBLK = 5
CAP = 2
BAND = 4
TPD = 4
KB = 20
NODES = 655360
N_ROW = 16
N_COL = 64


def need_counts(key):
    key_count, key_full = jax.random.split(key)
    counts = jax.random.randint(key_count, (N_ROW, N_COL, N_ROW), 1, CAP + 1)
    full_reader = jax.random.randint(key_full, (N_ROW, N_COL, 1), 0, N_ROW)
    readers = jnp.arange(N_ROW, dtype=jnp.int32)[None, None, :]
    return jnp.where(readers == full_reader, CAP, counts).astype(jnp.int32)


def draw_send_blocks(key, part):
    counts = need_counts(key)
    key = jax.random.fold_in(key, 3)
    start = jax.random.randint(key, (N_ROW, N_COL, N_ROW, 1), 0, NBLK)
    slot_pos = jnp.arange(CAP, dtype=jnp.int32)[None, None, None, :]
    block_ids = (start + slot_pos) % NBLK
    return jnp.where(slot_pos < counts[..., None], block_ids, -1).astype(jnp.int32)


def draw_tile_slots(key, part):
    counts = need_counts(key)
    key = jax.random.fold_in(key, 5)
    key_row, key_slot = jax.random.split(key)
    shape = (N_ROW, N_COL, KB, TPD)
    source_row = jax.random.randint(key_row, shape, 0, N_ROW)
    reader = jnp.arange(N_ROW, dtype=jnp.int32)[:, None, None, None]
    column = jnp.arange(N_COL, dtype=jnp.int32)[None, :, None, None]
    live_count = counts[source_row, column, reader]
    within = jax.random.randint(key_slot, shape, 0, live_count)
    return (source_row * CAP + within).astype(jnp.int32)


def draw_tile_count(key, part):
    key = jax.random.fold_in(key, 7)
    key_count, key_full = jax.random.split(key)
    counts = jax.random.randint(key_count, (N_ROW, N_COL, KB), 1, TPD + 1)
    full_block = jax.random.randint(key_full, (N_ROW, N_COL, 1), 0, KB)
    positions = jnp.arange(KB, dtype=jnp.int32)[None, None, :]
    return jnp.where(positions == full_block, TPD, counts).astype(jnp.int32)


def block_scale(own_key, shape, pieces, low, high):
    factor_of = 1.0
    for position, blocks in pieces:
        steps = jax.random.uniform(jax.random.fold_in(jax.random.fold_in(own_key, 6), position), (blocks,), jnp.float32, low / len(pieces), high / len(pieces))
        factor_of = factor_of * jnp.repeat(jnp.exp(steps), shape[position] // blocks).reshape((-1,) + (1,) * (len(shape) - 1 - position))
    return factor_of


def centred(own_key, extent, deviation, bound, cuts=(), held_as=jnp.bfloat16):
    drawn = jax.random.normal(own_key, extent, jnp.float32) * deviation
    if len(cuts) > 0:
        drawn = block_scale(own_key, extent, cuts, -0.22, 0.18) * drawn
    return jnp.clip(drawn, min=-bound, max=bound).astype(held_as)


def setup_inputs(seed: int = 0) -> dict:
    keys = jax.random.split(jax.random.key(seed), 9)
    return {
        "features": centred(keys[0], (NODES, F), 1.0, 6.0, ((0, 1024),)),
        "send_blocks": draw_send_blocks(jax.random.fold_in(keys[8], 71), 0),
        "tile_slots": draw_tile_slots(jax.random.fold_in(keys[8], 71), 0),
        "tile_count": draw_tile_count(jax.random.fold_in(keys[8], 71), 0),
        "adjacency": centred(keys[4], (N_ROW, N_COL, KB, TILE, TPD * TILE), (TPD * TILE) ** -0.5, 0.25, ((0, 16), (1, 64))),
        "w_self": centred(keys[5], (F, H), F ** -0.5, 0.5),
        "w_neigh": centred(keys[6], (F, H), F ** -0.5, 0.5),
        "bias": centred(keys[7], (H,), 0.5, 3.0, (), jnp.float32),
    }


def reference(features, send_blocks, tile_slots, tile_count, adjacency, w_self, w_neigh, bias):
    blocks = features.reshape(N_ROW, N_COL, NBLK, TILE, F)
    row_ids = jnp.arange(N_ROW, dtype=jnp.int32)
    tile_ids = jnp.arange(TPD, dtype=jnp.int32)

    def owner_rows(flat_index):
        r = flat_index // N_COL
        c = flat_index % N_COL
        summed = jnp.zeros((NBLK * TILE, F), jnp.float32)
        for k in range(BAND):
            src_col = (c - k) % N_COL
            block_ids = send_blocks[:, src_col, r, :]
            col_blocks = blocks[:, src_col]
            picked = col_blocks[row_ids[:, None], jnp.clip(block_ids, 0, NBLK - 1)]
            picked = jnp.where((block_ids >= 0)[:, :, None, None], picked, jnp.zeros((), jnp.bfloat16))
            source = picked.reshape(N_ROW * CAP, TILE, F)
            slot_ids = tile_slots[r, src_col][k * NBLK:(k + 1) * NBLK]
            counts = tile_count[r, src_col][k * NBLK:(k + 1) * NBLK]
            live_mask = tile_ids[None, :] < counts[:, None]
            operand = jnp.where(live_mask[:, :, None, None], source[slot_ids], jnp.zeros((), jnp.bfloat16))
            operand = operand.reshape(NBLK, TPD * TILE, F)
            adjacent = adjacency[r, src_col][k * NBLK:(k + 1) * NBLK]
            product = jnp.einsum('bim,bmf->bif', adjacent.astype(jnp.float32), operand.astype(jnp.float32))
            summed = summed + product.reshape(NBLK * TILE, F)
        aggregate = summed.astype(jnp.bfloat16)
        own_rows = blocks[r, c].reshape(NBLK * TILE, F)
        pre_act = jnp.dot(own_rows, w_self, preferred_element_type=jnp.float32)
        pre_act = pre_act + jnp.dot(aggregate, w_neigh, preferred_element_type=jnp.float32) + bias
        return jax.nn.relu(pre_act).astype(jnp.bfloat16)

    result = lax.map(owner_rows, jnp.arange(N_ROW * N_COL, dtype=jnp.int32))
    return result.reshape(NODES, H)
```

```python
import functools

import jax
import jax.numpy as jnp
from jax import lax
from jax.experimental import pallas as pl
from jax.experimental.pallas import tpu as pltpu
from jax.sharding import PartitionSpec as P

SCALE = 8192.0


def passed_along(value, axis, steps):
    count = lax.axis_size(axis)
    pairs = [(source, (source + steps) % count) for source in range(count)]
    return lax.ppermute(value, axis, pairs)


def tile_products(first, count, per_dst, rows, slots_ref, place_ref, x_ref, adj_ref, write):
    for b in range(count):
        tiles = []
        for j in range(per_dst):
            slot = slots_ref[(first + b) * per_dst + j]
            start = pl.multiple_of(place_ref[jnp.maximum(slot, 0)], 16)
            tile = x_ref[pl.ds(start, rows), :]
            tiles.append(jnp.where(slot >= 0, tile, jnp.zeros_like(tile)))
        operand = jnp.concatenate(tiles, axis=0)
        product = jnp.dot(adj_ref[first + b], operand, preferred_element_type=jnp.float32)
        write(b, product * (1.0 / SCALE))


def last_kernel(own, band, per_dst, rows, slots_ref, place_ref, x_ref, adj_ref, far_ref):
    def write(b, product):
        far_ref[b * rows : (b + 1) * rows, :] = product.astype(far_ref.dtype)

    tile_products((band - 1) * own, own, per_dst, rows, slots_ref, place_ref, x_ref, adj_ref, write)


def rest_kernel(own, band, per_dst, rows, slots_ref, place_ref, x_ref, adj_ref, mine_ref, near_ref, mid_ref):
    for k, out_ref in ((1, near_ref), (2, mid_ref), (0, mine_ref)):

        def write(b, product, out_ref=out_ref):
            out_ref[b * rows : (b + 1) * rows, :] = product.astype(out_ref.dtype)

        tile_products(k * own, own, per_dst, rows, slots_ref, place_ref, x_ref, adj_ref, write)


def final_kernel(self_ref, mine_ref, near_ref, far_ref, w_ref, bias_ref, out_ref):
    summed = mine_ref[...] + near_ref[...].astype(jnp.float32) + far_ref[...].astype(jnp.float32)
    pre_act = jnp.dot(summed.astype(jnp.bfloat16), w_ref[...], preferred_element_type=jnp.float32)
    pre_act = pre_act + self_ref[...] + bias_ref[...]
    out_ref[...] = jnp.maximum(pre_act, 0.0).astype(out_ref.dtype)


def shards(features, send_blocks, tile_slots, tile_count, adjacency, w_self, w_neigh, bias):
    row_count = lax.axis_size("row")
    readers, cap = send_blocks.shape[2:]
    tile_rows = adjacency.shape[3]
    per_dst = tile_slots.shape[3]
    nodes, width = features.shape
    own = nodes // tile_rows
    band = adjacency.shape[2] // own
    assert band == 4

    scaled = (features.astype(jnp.float32) * SCALE).astype(jnp.float16)
    listed = jnp.pad(send_blocks[0, 0].astype(jnp.float16), ((0, 0), (0, width - cap)))
    held = nodes + readers
    got = lax.all_gather(jnp.concatenate([scaled, listed], axis=0), "row", axis=0, tiled=True)
    reader = lax.axis_index("row")
    need = lax.dynamic_slice(got.reshape(row_count, held, width), (0, nodes + reader, 0), (row_count, 1, cap))
    need = jnp.clip(need.reshape(row_count, cap).astype(jnp.int32), 0, own - 1)
    place = jnp.arange(row_count, dtype=jnp.int32)[:, None] * held + need * tile_rows
    place = place.reshape(row_count * cap)
    live = jnp.arange(per_dst, dtype=jnp.int32)[None, :] < tile_count[0, 0][:, None]
    slots = jnp.where(live, tile_slots[0, 0], -1).reshape(-1)
    source = got.astype(jnp.bfloat16)
    adjacent = adjacency[0, 0]

    smem = pl.BlockSpec(memory_space=pltpu.SMEM)
    vmem = pl.BlockSpec(memory_space=pltpu.VMEM)
    part = functools.partial
    tile_flops = 2 * tile_rows * tile_rows * per_dst * width
    far = pl.pallas_call(
        part(last_kernel, own, band, per_dst, tile_rows),
        out_shape=jax.ShapeDtypeStruct((nodes, width), jnp.bfloat16),
        in_specs=[smem, smem, vmem, vmem],
        out_specs=vmem,
        cost_estimate=pl.CostEstimate(flops=own * tile_flops, bytes_accessed=2**20, transcendentals=0),
    )(slots, place, source, adjacent)
    far = passed_along(far, "col", 1)
    mine, near, mid = pl.pallas_call(
        part(rest_kernel, own, band, per_dst, tile_rows),
        out_shape=[
            jax.ShapeDtypeStruct((nodes, width), jnp.float32),
            jax.ShapeDtypeStruct((nodes, width), jnp.bfloat16),
            jax.ShapeDtypeStruct((nodes, width), jnp.float32),
        ],
        in_specs=[smem, smem, vmem, vmem],
        out_specs=[vmem, vmem, vmem],
        cost_estimate=pl.CostEstimate(flops=3 * own * tile_flops, bytes_accessed=3 * 2**20, transcendentals=0),
    )(slots, place, source, adjacent)
    near = passed_along(near, "col", 1)
    far = passed_along((far.astype(jnp.float32) + mid).astype(jnp.bfloat16), "col", 2)
    own_part = jnp.dot(features, w_self, preferred_element_type=jnp.float32)
    return pl.pallas_call(
        final_kernel,
        out_shape=jax.ShapeDtypeStruct((nodes, w_self.shape[1]), jnp.bfloat16),
        in_specs=[vmem] * 6,
        out_specs=vmem,
    )(own_part, mine, near, far, w_neigh, bias.reshape(1, -1))


def solution(mesh):
    return jax.shard_map(
        shards,
        mesh=mesh,
        in_specs=(
            P(("row", "col"), None),
            P("row", "col", None, None),
            P("row", "col", None, None),
            P("row", "col", None),
            P("row", "col", None, None, None),
            P(),
            P(),
            P(),
        ),
        out_specs=P(("row", "col"), None),
        check_vma=False,
    )
```

```python
import functools

import jax
import jax.numpy as jnp
from jax import lax
from jax.experimental import pallas as pl
from jax.experimental.pallas import tpu as pltpu
from jax.sharding import PartitionSpec as P

SCALE = 8192.0
PART_SCALE = 32.0
VMEM_LIMIT = 8 * 2**20


def passed_along(value, axis, steps):
    count = lax.axis_size(axis)
    pairs = [(source, (source + steps) % count) for source in range(count)]
    return lax.ppermute(value, axis, pairs)


def pack_kernel(last, features_ref, listed_ref, slots_ref, counts_ref, adj_ref, out_ref, plan_ref, adj_out, listed, slots, counts, turned, arrived):
    nodes = features_ref.shape[0]
    cap, readers = listed_ref.shape
    per_dst, blocks = slots_ref.shape
    copies = []
    for source, target in (
        (listed_ref, listed),
        (slots_ref, slots),
        (counts_ref, counts),
        (features_ref, out_ref.at[pl.ds(0, nodes)]),
        (adj_ref.at[pl.ds(last, blocks - last)], adj_out),
    ):
        copy = pltpu.make_async_copy(source, target, arrived.at[len(copies)])
        copy.start()
        copies.append(copy)
    turned[...] = jnp.zeros_like(turned)
    for copy in copies[:3]:
        copy.wait()
    plan_ref[:per_dst, :] = slots[...]
    plan_ref[per_dst:, :] = counts[...]
    turned[:cap, :readers] = listed[...].astype(jnp.float32)
    out_ref[nodes:, :] = jnp.transpose(turned[...])[:readers, :].astype(out_ref.dtype)
    for copy in copies[3:]:
        copy.wait()


def band_kernel(ks, first, own, rows, held, plan_ref, need_ref, x_ref, adj_ref, *rest):
    *outs, operand = rest
    per_dst = plan_ref.shape[0] - 1
    cap = need_ref.shape[1]
    for k, out_ref in zip(ks, outs, strict=True):
        for b in range(own):
            block = k * own + b
            for j in range(per_dst):
                slot = plan_ref[j, block]
                owner = lax.div(slot, cap)
                wanted = jnp.clip(need_ref[owner, lax.rem(slot, cap)], 0, own - 1)
                start = pl.multiple_of(owner * held + wanted * rows, 16)
                tile = x_ref[pl.ds(start, rows), :]
                tile = jnp.where(j < plan_ref[per_dst, block], tile, jnp.zeros_like(tile))
                operand[b, j * rows : (j + 1) * rows, :] = tile
        for b in range(own):
            product = jnp.dot(adj_ref[k * own + b - first], operand[b], preferred_element_type=jnp.float32)
            out_ref[b * rows : (b + 1) * rows, :] = product * (PART_SCALE / SCALE)


def final_kernel(self_ref, *rest):
    *parts, w_ref, bias_ref, out_ref = rest
    summed = parts[0][...]
    for part in parts[1:]:
        summed = summed + part[...]
    aggregate = (summed * (1.0 / PART_SCALE)).astype(jnp.bfloat16)
    pre_act = jnp.dot(aggregate, w_ref[...], preferred_element_type=jnp.float32)
    pre_act = pre_act + self_ref[...] + bias_ref[...]
    out_ref[...] = jnp.maximum(pre_act, 0.0).astype(out_ref.dtype)


def in_hbm(value):
    return pltpu.with_memory_space_constraint(value, pltpu.HBM)


def in_vmem(value):
    return pltpu.with_memory_space_constraint(value, pltpu.VMEM)


def shards(features, send_blocks, tile_slots, tile_count, adjacency, w_self, w_neigh, bias):
    row_count = lax.axis_size("row")
    readers, cap = send_blocks.shape[2:]
    rows = adjacency.shape[3]
    per_dst = tile_slots.shape[3]
    nodes, width = features.shape
    own = nodes // rows
    band = adjacency.shape[2] // own
    assert band == 4
    smem = pl.BlockSpec(memory_space=pltpu.SMEM)
    vmem = pl.BlockSpec(memory_space=pltpu.VMEM)
    anywhere = pl.BlockSpec(memory_space=pl.ANY)
    params = pltpu.CompilerParams(vmem_limit_bytes=VMEM_LIMIT)

    held = nodes + readers
    last = (band - 1) * own
    adjacent = adjacency[0, 0]
    packed, plan, adjacent_last = pl.pallas_call(
        functools.partial(pack_kernel, last),
        out_shape=[
            pltpu.VMEM((held, width), jnp.bfloat16),
            pltpu.VMEM((per_dst + 1, band * own), jnp.int32),
            pltpu.VMEM((own, *adjacent.shape[1:]), jnp.bfloat16),
        ],
        in_specs=[anywhere] * 5,
        out_specs=[vmem] * 3,
        scratch_shapes=[
            pltpu.VMEM((cap, readers), jnp.int32),
            pltpu.VMEM((per_dst, band * own), jnp.int32),
            pltpu.VMEM((1, band * own), jnp.int32),
            pltpu.VMEM((width, width), jnp.float32),
            pltpu.SemaphoreType.DMA((5,)),
        ],
        compiler_params=params,
    )(in_hbm(features), in_hbm(send_blocks[0, 0].T), in_hbm(tile_slots[0, 0].T), in_hbm(tile_count[0]), in_hbm(adjacent))
    sent = (packed.astype(jnp.float32) * SCALE).astype(jnp.float16)
    got = lax.all_gather(sent, "row", axis=0, tiled=True)
    source = got.astype(jnp.bfloat16)
    reader = lax.axis_index("row")
    need = lax.dynamic_slice(source.reshape(row_count, held, width), (0, nodes + reader, 0), (row_count, 1, cap))
    need = (need.reshape(row_count, cap).astype(jnp.float32) * (1.0 / SCALE)).astype(jnp.int32)
    tile_flops = 2 * rows * rows * per_dst * width

    def products(ks, matrices, first):
        count = len(ks) * own
        return pl.pallas_call(
            functools.partial(band_kernel, ks, first, own, rows, held),
            out_shape=[pltpu.VMEM((nodes, width), jnp.float32)] * len(ks),
            in_specs=[smem, smem, vmem, vmem],
            out_specs=[vmem] * len(ks),
            scratch_shapes=[pltpu.VMEM((own, per_dst * rows, width), jnp.bfloat16)],
            compiler_params=params,
            cost_estimate=pl.CostEstimate(flops=count * tile_flops, bytes_accessed=len(ks) * 2**20, transcendentals=0),
        )(plan, need, in_vmem(source), in_vmem(matrices))

    (far,) = products((3,), adjacent_last, last)
    far = passed_along(far.astype(jnp.float16), "col", 1)
    (near,) = products((1,), adjacent, 0)
    near = passed_along(near.astype(jnp.float16), "col", 1)
    mid, mine = products((2, 0), adjacent, 0)
    far = passed_along((far.astype(jnp.float32) + mid).astype(jnp.float16), "col", 2)
    parts = (mine, near.astype(jnp.float32), far.astype(jnp.float32))
    own_part = jnp.dot(features, w_self, preferred_element_type=jnp.float32)
    return pl.pallas_call(
        final_kernel,
        out_shape=jax.ShapeDtypeStruct((nodes, w_self.shape[1]), jnp.bfloat16),
        in_specs=[vmem] * (len(parts) + 3),
        out_specs=vmem,
        compiler_params=params,
    )(in_vmem(own_part), *[in_vmem(p) for p in parts], in_vmem(w_neigh), in_vmem(bias.reshape(1, -1)))


def solution(mesh):
    return jax.shard_map(
        shards,
        mesh=mesh,
        in_specs=(
            P(("row", "col"), None),
            P("row", "col", None, None),
            P("row", "col", None, None),
            P("row", "col", None),
            P("row", "col", None, None, None),
            P(),
            P(),
            P(),
        ),
        out_specs=P(("row", "col"), None),
        check_vma=False,
    )
```

```python
import functools

import jax
import jax.numpy as jnp
from jax import lax
from jax.experimental import pallas as pl
from jax.experimental.pallas import tpu as pltpu
from jax.sharding import PartitionSpec as P

SCALE = 8192.0
PART_SCALE = 32.0
VMEM_LIMIT = 8 * 2**20
LINE = 8


def passed_along(value, axis, steps, chosen=lambda source: True):
    count = lax.axis_size(axis)
    pairs = [(source, (source + steps) % count) for source in range(count) if chosen(source)]
    return lax.ppermute(value, axis, pairs)


def pack_kernel(last, features_ref, listed_ref, slots_ref, counts_ref, adj_ref, out_ref, plan_ref, adj_out, listed, slots, counts, turned, arrived):
    nodes = features_ref.shape[0]
    cap, readers = listed_ref.shape
    per_dst, blocks = slots_ref.shape
    copies = []
    for source, target in (
        (listed_ref, listed),
        (slots_ref, slots),
        (counts_ref, counts),
        (features_ref, out_ref.at[pl.ds(0, nodes)]),
        (adj_ref.at[pl.ds(last, blocks - last)], adj_out),
    ):
        copy = pltpu.make_async_copy(source, target, arrived.at[len(copies)])
        copy.start()
        copies.append(copy)
    turned[...] = jnp.zeros_like(turned)
    for copy in copies[:3]:
        copy.wait()
    plan_ref[:per_dst, :] = slots[...]
    plan_ref[per_dst:, :] = counts[...]
    turned[:cap, :readers] = listed[...].astype(jnp.float32)
    out_ref[nodes:, :] = jnp.transpose(turned[...])[:readers, :].astype(out_ref.dtype)
    for copy in copies[3:]:
        copy.wait()


def band_kernel(ks, first, own, rows, held, plan_ref, need_ref, x_ref, adj_ref, *outs):
    per_dst = plan_ref.shape[0] - 1
    cap = need_ref.shape[1]
    for k, out_ref in zip(ks, outs, strict=True):
        for b in range(own):
            block = k * own + b
            tiles = []
            for j in range(per_dst):
                slot = plan_ref[j, block]
                owner = lax.div(slot, cap)
                wanted = jnp.clip(need_ref[owner, lax.rem(slot, cap)], 0, own - 1)
                start = pl.multiple_of(owner * held + wanted * rows, 16)
                tile = x_ref[pl.ds(start, rows), :]
                tiles.append(jnp.where(j < plan_ref[per_dst, block], tile, jnp.zeros_like(tile)))
            operand = jnp.concatenate(tiles, axis=0)
            product = jnp.dot(adj_ref[block - first], operand, preferred_element_type=jnp.float32)
            out_ref[b * rows : (b + 1) * rows, :] = product * (PART_SCALE / SCALE)


def final_kernel(self_ref, *rest):
    *parts, w_ref, bias_ref, out_ref = rest
    summed = parts[0][...]
    for part in parts[1:]:
        summed = summed + part[...]
    aggregate = (summed * (1.0 / PART_SCALE)).astype(jnp.bfloat16)
    pre_act = jnp.dot(aggregate, w_ref[...], preferred_element_type=jnp.float32)
    pre_act = pre_act + self_ref[...] + bias_ref[...]
    out_ref[...] = jnp.maximum(pre_act, 0.0).astype(out_ref.dtype)


def in_hbm(value):
    return pltpu.with_memory_space_constraint(value, pltpu.HBM)


def in_vmem(value):
    return pltpu.with_memory_space_constraint(value, pltpu.VMEM)


def shards(features, send_blocks, tile_slots, tile_count, adjacency, w_self, w_neigh, bias):
    row_count = lax.axis_size("row")
    readers, cap = send_blocks.shape[2:]
    rows = adjacency.shape[3]
    per_dst = tile_slots.shape[3]
    nodes, width = features.shape
    own = nodes // rows
    band = adjacency.shape[2] // own
    assert band == 4
    smem = pl.BlockSpec(memory_space=pltpu.SMEM)
    vmem = pl.BlockSpec(memory_space=pltpu.VMEM)
    anywhere = pl.BlockSpec(memory_space=pl.ANY)
    params = pltpu.CompilerParams(vmem_limit_bytes=VMEM_LIMIT)

    held = nodes + readers
    last = (band - 1) * own
    adjacent = adjacency[0, 0]
    packed, plan, adjacent_last = pl.pallas_call(
        functools.partial(pack_kernel, last),
        out_shape=[
            pltpu.VMEM((held, width), jnp.bfloat16),
            pltpu.VMEM((per_dst + 1, band * own), jnp.int32),
            pltpu.VMEM((own, *adjacent.shape[1:]), jnp.bfloat16),
        ],
        in_specs=[anywhere] * 5,
        out_specs=[vmem] * 3,
        scratch_shapes=[
            pltpu.VMEM((cap, readers), jnp.int32),
            pltpu.VMEM((per_dst, band * own), jnp.int32),
            pltpu.VMEM((1, band * own), jnp.int32),
            pltpu.VMEM((width, width), jnp.float32),
            pltpu.SemaphoreType.DMA((5,)),
        ],
        compiler_params=params,
    )(in_hbm(features), in_hbm(send_blocks[0, 0].T), in_hbm(tile_slots[0, 0].T), in_hbm(tile_count[0]), in_hbm(adjacent))
    sent = (packed.astype(jnp.float32) * SCALE).astype(jnp.float16)
    got = lax.all_gather(sent, "row", axis=0, tiled=True)
    source = got.astype(jnp.bfloat16)
    reader = lax.axis_index("row")
    need = lax.dynamic_slice(source.reshape(row_count, held, width), (0, nodes + reader, 0), (row_count, 1, cap))
    need = (need.reshape(row_count, cap).astype(jnp.float32) * (1.0 / SCALE)).astype(jnp.int32)
    tile_flops = 2 * rows * rows * per_dst * width

    def products(ks, matrices, first, need):
        count = len(ks) * own
        return pl.pallas_call(
            functools.partial(band_kernel, ks, first, own, rows, held),
            out_shape=[pltpu.VMEM((nodes, width), jnp.float32)] * len(ks),
            in_specs=[smem, smem, vmem, vmem],
            out_specs=[vmem] * len(ks),
            compiler_params=params,
            cost_estimate=pl.CostEstimate(flops=count * tile_flops, bytes_accessed=len(ks) * 2**20, transcendentals=0),
        )(plan, need, in_vmem(source), in_vmem(matrices))

    (far,) = products((3,), adjacent_last, last, need)
    far = far.astype(jnp.float16)
    stayed = passed_along(far, "col", 1, lambda source: source % LINE < LINE - 1)
    left = passed_along(far, "col", 1, lambda source: source % LINE == LINE - 1)
    (near,) = products((1,), adjacent, 0, need)
    near = passed_along(near.astype(jnp.float16), "col", 1)
    mid, mine = products((2, 0), adjacent, 0, need)
    pair = (stayed.astype(jnp.float32) + mid).astype(jnp.float16)
    crossing = passed_along(pair, "col", 2, lambda source: source % LINE >= LINE - 2)
    own_part = jnp.dot(features, w_self, preferred_element_type=jnp.float32)
    left, pair = lax.optimization_barrier((left, pair))
    pair = (stayed.astype(jnp.float32) + left.astype(jnp.float32) + mid).astype(jnp.float16)
    inside = passed_along(pair, "col", 2, lambda source: source % LINE < LINE - 2)
    parts = (mine, near.astype(jnp.float32), crossing.astype(jnp.float32) + inside.astype(jnp.float32))
    return pl.pallas_call(
        final_kernel,
        out_shape=jax.ShapeDtypeStruct((nodes, w_self.shape[1]), jnp.bfloat16),
        in_specs=[vmem] * (len(parts) + 3),
        out_specs=vmem,
        compiler_params=params,
    )(in_vmem(own_part), *[in_vmem(p) for p in parts], in_vmem(w_neigh), in_vmem(bias.reshape(1, -1)))


def solution(mesh):
    return jax.shard_map(
        shards,
        mesh=mesh,
        in_specs=(
            P(("row", "col"), None),
            P("row", "col", None, None),
            P("row", "col", None, None),
            P("row", "col", None),
            P("row", "col", None, None, None),
            P(),
            P(),
            P(),
        ),
        out_specs=P(("row", "col"), None),
        check_vma=False,
    )
```

```python
import functools

import jax
import jax.numpy as jnp
from jax import lax
from jax.experimental import pallas as pl
from jax.experimental.pallas import tpu as pltpu
from jax.sharding import PartitionSpec as P

SCALE = 8192.0
PART_SCALE = 32.0
VMEM_LIMIT = 8 * 2**20
LINE = 8


def passed_along(value, axis, steps, chosen=lambda source: True):
    count = lax.axis_size(axis)
    pairs = [(source, (source + steps) % count) for source in range(count) if chosen(source)]
    return lax.ppermute(value, axis, pairs)


def pack_kernel(last, features_ref, listed_ref, slots_ref, counts_ref, adj_ref, out_ref, plan_ref, adj_out, listed, slots, counts, turned, arrived):
    nodes = features_ref.shape[0]
    cap, readers = listed_ref.shape
    per_dst, blocks = slots_ref.shape
    copies = []
    for source, target in (
        (listed_ref, listed),
        (slots_ref, slots),
        (counts_ref, counts),
        (features_ref, out_ref.at[pl.ds(0, nodes)]),
        (adj_ref.at[pl.ds(last, blocks - last)], adj_out),
    ):
        copy = pltpu.make_async_copy(source, target, arrived.at[len(copies)])
        copy.start()
        copies.append(copy)
    turned[...] = jnp.zeros_like(turned)
    for copy in copies[:3]:
        copy.wait()
    plan_ref[:per_dst, :] = slots[...]
    plan_ref[per_dst:, :] = counts[...]
    turned[:cap, :readers] = listed[...].astype(jnp.float32)
    out_ref[nodes:, :] = jnp.transpose(turned[...])[:readers, :].astype(out_ref.dtype)
    for copy in copies[3:]:
        copy.wait()


def band_kernel(ks, first, own, rows, held, cap, plan_ref, need_ref, x_ref, adj_ref, *outs):
    per_dst = plan_ref.shape[0] - 1
    for k, out_ref in zip(ks, outs, strict=True):
        for b in range(own):
            block = k * own + b
            tiles = []
            for j in range(per_dst):
                slot = plan_ref[j, block]
                owner = lax.div(slot, cap)
                wanted = jnp.clip(need_ref[owner, lax.rem(slot, cap)], 0, own - 1)
                start = pl.multiple_of(owner * held + wanted * rows, 16)
                tile = x_ref[pl.ds(start, rows), :]
                tiles.append(jnp.where(j < plan_ref[per_dst, block], tile, jnp.zeros_like(tile)))
            operand = jnp.concatenate(tiles, axis=0)
            product = jnp.dot(adj_ref[block - first], operand, preferred_element_type=jnp.float32)
            out_ref[b * rows : (b + 1) * rows, :] = product * (PART_SCALE / SCALE)


def final_kernel(self_ref, *rest):
    *parts, w_ref, bias_ref, out_ref = rest
    summed = parts[0][...]
    for part in parts[1:]:
        summed = summed + part[...]
    aggregate = (summed * (1.0 / PART_SCALE)).astype(jnp.bfloat16)
    pre_act = jnp.dot(aggregate, w_ref[...], preferred_element_type=jnp.float32)
    pre_act = pre_act + self_ref[...] + bias_ref[...]
    out_ref[...] = jnp.maximum(pre_act, 0.0).astype(out_ref.dtype)


def in_hbm(value):
    return pltpu.with_memory_space_constraint(value, pltpu.HBM)


def in_vmem(value):
    return pltpu.with_memory_space_constraint(value, pltpu.VMEM)


def shards(features, send_blocks, tile_slots, tile_count, adjacency, w_self, w_neigh, bias):
    row_count = lax.axis_size("row")
    readers, cap = send_blocks.shape[2:]
    rows = adjacency.shape[3]
    per_dst = tile_slots.shape[3]
    nodes, width = features.shape
    own = nodes // rows
    band = adjacency.shape[2] // own
    assert band == 4
    smem = pl.BlockSpec(memory_space=pltpu.SMEM)
    vmem = pl.BlockSpec(memory_space=pltpu.VMEM)
    anywhere = pl.BlockSpec(memory_space=pl.ANY)
    params = pltpu.CompilerParams(vmem_limit_bytes=VMEM_LIMIT)

    held = nodes + readers
    last = (band - 1) * own
    adjacent = adjacency[0, 0]
    packed, plan, adjacent_last = pl.pallas_call(
        functools.partial(pack_kernel, last),
        out_shape=[
            pltpu.VMEM((held, width), jnp.bfloat16),
            pltpu.VMEM((per_dst + 1, band * own), jnp.int32),
            pltpu.VMEM((own, *adjacent.shape[1:]), jnp.bfloat16),
        ],
        in_specs=[anywhere] * 5,
        out_specs=[vmem] * 3,
        scratch_shapes=[
            pltpu.VMEM((cap, readers), jnp.int32),
            pltpu.VMEM((per_dst, band * own), jnp.int32),
            pltpu.VMEM((1, band * own), jnp.int32),
            pltpu.VMEM((width, width), jnp.float32),
            pltpu.SemaphoreType.DMA((5,)),
        ],
        compiler_params=params,
    )(in_hbm(features), in_hbm(send_blocks[0, 0].T), in_hbm(tile_slots[0, 0].T), in_hbm(tile_count[0]), in_hbm(adjacent))
    sent = (packed.astype(jnp.float32) * SCALE).astype(jnp.float16)
    got = lax.all_gather(sent, "row", axis=0, tiled=True)
    source = got.astype(jnp.bfloat16)
    reader = lax.axis_index("row")
    need = lax.dynamic_slice(source.reshape(row_count, held, width), (0, nodes + reader, 0), (row_count, 1, width))
    need = (need.reshape(row_count, width).astype(jnp.float32) * (1.0 / SCALE)).astype(jnp.int32)
    tile_flops = 2 * rows * rows * per_dst * width

    def products(ks, matrices, first, need):
        count = len(ks) * own
        return pl.pallas_call(
            functools.partial(band_kernel, ks, first, own, rows, held, cap),
            out_shape=[pltpu.VMEM((nodes, width), jnp.float32)] * len(ks),
            in_specs=[smem, smem, vmem, vmem],
            out_specs=[vmem] * len(ks),
            compiler_params=params,
            cost_estimate=pl.CostEstimate(flops=count * tile_flops, bytes_accessed=len(ks) * 2**20, transcendentals=0),
        )(plan, need, in_vmem(source), in_vmem(matrices))

    (far,) = products((3,), adjacent_last, last, need)
    far = far.astype(jnp.float16)
    stayed = passed_along(far, "col", 1, lambda source: source % LINE < LINE - 1)
    left = passed_along(far, "col", 1, lambda source: source % LINE == LINE - 1)
    (near,) = products((1,), adjacent, 0, need)
    near = passed_along(near.astype(jnp.float16), "col", 1)
    mid, mine = products((2, 0), adjacent, 0, need)
    pair = (stayed.astype(jnp.float32) + mid).astype(jnp.float16)
    crossing = passed_along(pair, "col", 2, lambda source: source % LINE >= LINE - 2)
    own_part = jnp.dot(features, w_self, preferred_element_type=jnp.float32)
    left, pair = lax.optimization_barrier((left, pair))
    pair = (stayed.astype(jnp.float32) + left.astype(jnp.float32) + mid).astype(jnp.float16)
    inside = passed_along(pair, "col", 2, lambda source: source % LINE < LINE - 2)
    parts = (mine, near.astype(jnp.float32), crossing.astype(jnp.float32) + inside.astype(jnp.float32))
    return pl.pallas_call(
        final_kernel,
        out_shape=jax.ShapeDtypeStruct((nodes, w_self.shape[1]), jnp.bfloat16),
        in_specs=[vmem] * (len(parts) + 3),
        out_specs=vmem,
        compiler_params=params,
    )(in_vmem(own_part), *[in_vmem(p) for p in parts], in_vmem(w_neigh), in_vmem(bias.reshape(1, -1)))


def solution(mesh):
    return jax.shard_map(
        shards,
        mesh=mesh,
        in_specs=(
            P(("row", "col"), None),
            P("row", "col", None, None),
            P("row", "col", None, None),
            P("row", "col", None),
            P("row", "col", None, None, None),
            P(),
            P(),
            P(),
        ),
        out_specs=P(("row", "col"), None),
        check_vma=False,
    )
```
